32 devices in a mesh: req: 4 (over z), seq: 8 (over y, x, core).
Axes of the slice: x: 2, y: 2, z: 4, core: 2. Of those that a mesh axis runs over, the one named last changes fastest.
Arguments:
- hidden_in: bfloat16 [8, 256, 2048], P('req', 'seq'), may hold values from -6 to 6
- norm_gain: float32 [2048], replicated, may hold values from 0.1 to 1.9
- w_query: bfloat16 [2048, 1024], P(('req', 'seq')), may hold values from -0.125 to 0.125
- w_key: bfloat16 [2048, 512], P(('req', 'seq')), may hold values from -0.3125 to 0.3125
- w_value: bfloat16 [2048, 512], P(('req', 'seq')), may hold values from -0.125 to 0.125
- cache_keys: bfloat16 [8, 2048, 512], P('req', 'seq'), may hold values from -525 to 525
- cache_values: bfloat16 [8, 2048, 512], P('req', 'seq'), may hold values from -6 to 6
- cache_lengths: int32 [8], P('req'), may hold values from 1 to 2048, as said below
Outputs:
- attended: bfloat16 [8, 256, 1024], P('req', 'seq')
- new_keys: bfloat16 [8, 256, 512], P('req', 'seq')
- new_values: bfloat16 [8, 256, 512], P('req', 'seq')
The draws below stay inside these ranges and needn't reach their ends.
Inputs may be any that keep to these rules, and one draw needn't show every extreme that they name: `cache_lengths`: some request's cache holds exactly 2048 positions.
All inputs are finite; a program needn't handle non-finite values.
Results may differ from the reference program's by a relative error of at most 0.034.
Values may be sent and summed in bfloat16 or wider, within the bound.
A program may use at most 128 MiB of HBM per device.

```python
import jax
import jax.numpy as jnp
from jax import lax

D = 2048
HEADS = 4
KV_HEADS = 2
HEAD = 256
CSLICE = 32
CACHE_DEV = 256
REQS = 8
SPAN = 256
CTX = 2048
N_SEQ = 8


def draw_cache_lengths(key, part):
    first_key, second_key = jax.random.split(key)
    lengths = jax.random.randint(first_key, (REQS,), 1, CTX + 1)
    chosen = jax.random.randint(second_key, (), 0, REQS)
    return jnp.where(jnp.arange(REQS) == chosen, CTX, lengths).astype(jnp.int32)


def draw_cache_keys(key, part):
    split_keys = jax.random.split(key, 1)
    normal_rows = 2.5 * jax.random.normal(split_keys[0], (REQS, CTX, KV_HEADS * HEAD), jnp.float32)
    return jnp.clip(normal_rows, -15.0, 15.0).astype(jnp.bfloat16)


def shard_levels(stream_key, shape, cuts, low, top_value):
    def one(position, shards_of):
        heights = jax.random.uniform(jax.random.fold_in(jax.random.fold_in(stream_key, 6), position), (shards_of,), jnp.float32, low / len(cuts), top_value / len(cuts))
        return jnp.repeat(jnp.exp(heights), shape[position] // shards_of).reshape((-1,) + (1,) * (len(shape) - position - 1))

    factor_of = one(*cuts[0])
    for cut in cuts[1:]:
        factor_of = factor_of * one(*cut)
    return factor_of


def normal_values(stream_key, shape, scale, limit, cuts=(), kind=jnp.bfloat16):
    array = scale * jax.random.normal(stream_key, shape, jnp.float32)
    if cuts:
        array = array * shard_levels(stream_key, shape, cuts, -0.22, 0.18)
    return jnp.clip(array, -limit, limit).astype(kind)


def setup_inputs(seed: int = 0) -> dict:
    key_of = jax.random.split(jax.random.key(seed), 9)
    return {
        "hidden_in": normal_values(key_of[0], (REQS, SPAN, D), 1.0, 6.0, ((0, 4), (1, 8))),
        "norm_gain": jnp.clip(1.0 + 0.18 * jax.random.normal(key_of[1], (D,), jnp.float32), 0.1, 1.9),
        "w_query": normal_values(key_of[2], (D, HEADS * HEAD), D ** -0.5, 0.125, ((0, 32),)),
        "w_key": normal_values(key_of[3], (D, KV_HEADS * HEAD), (D // 6) ** -0.5, 0.3125, ((0, 32),)),
        "w_value": normal_values(key_of[4], (D, KV_HEADS * HEAD), D ** -0.5, 0.125, ((0, 32),)),
        "cache_keys": draw_cache_keys(jax.random.fold_in(key_of[8], 71), 0),
        "cache_values": normal_values(key_of[6], (REQS, CTX, KV_HEADS * HEAD), 1.0, 6.0, ((0, 4), (1, 8))),
        "cache_lengths": draw_cache_lengths(jax.random.fold_in(key_of[8], 71), 0),
    }


EPSILON = 1e-06
THETA = 1000042.0
MASKED = -1e+30

def tables(positions, head_size):
    half_size = head_size // 2
    frequency = THETA ** (-(jnp.arange(half_size, dtype=jnp.float32) * 2.0 / head_size))
    angles = positions.astype(jnp.float32)[..., None] * frequency
    return (jnp.cos(angles)[..., None, :], jnp.sin(angles)[..., None, :])

def rotate(values, cosine, sine_part):
    half_size = values.shape[-1] // 2
    first_half = values[..., :half_size]
    second_half = values[..., half_size:]
    return jnp.concatenate([first_half * cosine - second_half * sine_part, second_half * cosine + first_half * sine_part], axis=-1)

def reference(hidden_in, norm_gain, w_query, w_key, w_value, cache_keys, cache_values, cache_lengths):
    group_size = HEADS // KV_HEADS
    score_scale = HEAD ** (-0.5)
    inputs = hidden_in.astype(jnp.float32)
    normed = (inputs * lax.rsqrt(lax.optimization_barrier(jnp.mean(inputs * inputs, axis=-1, keepdims=True)) + EPSILON) * norm_gain).astype(jnp.bfloat16)
    flat_rows = normed.reshape(REQS * SPAN, D)
    query_raw = jnp.dot(flat_rows, w_query, preferred_element_type=jnp.float32).reshape(REQS, SPAN, HEADS, HEAD)
    key_raw = jnp.dot(flat_rows, w_key, preferred_element_type=jnp.float32).reshape(REQS, SPAN, KV_HEADS, HEAD)
    value_raw = jnp.dot(flat_rows, w_value, preferred_element_type=jnp.float32).reshape(REQS, SPAN, KV_HEADS * HEAD)
    positions = cache_lengths[:, None] + jnp.arange(SPAN, dtype=jnp.int32)[None, :]
    cosine, sine_part = tables(positions, HEAD)
    queries = rotate(query_raw, cosine, sine_part).astype(jnp.bfloat16)
    new_keys = rotate(key_raw, cosine, sine_part).reshape(REQS, SPAN, KV_HEADS * HEAD).astype(jnp.bfloat16)
    new_values = value_raw.astype(jnp.bfloat16)
    query_all = queries.astype(jnp.float32).reshape(REQS, SPAN, KV_HEADS, group_size, HEAD)
    span_index = jnp.arange(SPAN, dtype=jnp.int32)
    width_all = CACHE_DEV + CSLICE

    def block_terms(block_id):
        cache_start = block_id * CACHE_DEV
        new_start = block_id * CSLICE
        block_keys = jnp.concatenate([lax.dynamic_slice_in_dim(cache_keys, cache_start, CACHE_DEV, 1), lax.dynamic_slice_in_dim(new_keys, new_start, CSLICE, 1)], axis=1)
        block_values = jnp.concatenate([lax.dynamic_slice_in_dim(cache_values, cache_start, CACHE_DEV, 1), lax.dynamic_slice_in_dim(new_values, new_start, CSLICE, 1)], axis=1)
        key_all = block_keys.astype(jnp.float32).reshape(REQS, width_all, KV_HEADS, HEAD)
        value_all = block_values.astype(jnp.float32).reshape(REQS, width_all, KV_HEADS, HEAD)
        cache_pos = cache_start + jnp.arange(CACHE_DEV, dtype=jnp.int32)
        cache_live = cache_pos[None, None, :] < cache_lengths[:, None, None]
        new_pos = new_start + jnp.arange(CSLICE, dtype=jnp.int32)
        new_live = new_pos[None, None, :] <= span_index[None, :, None]
        live = jnp.concatenate([jnp.broadcast_to(cache_live, (REQS, SPAN, CACHE_DEV)), jnp.broadcast_to(new_live, (REQS, SPAN, CSLICE))], axis=2)[:, :, None, None, :]
        scores = jnp.einsum('rcgeh,rkgh->rcgek', query_all, key_all) * score_scale
        scores = jnp.where(live, scores, MASKED)
        block_max = lax.optimization_barrier(jnp.max(scores, axis=-1))
        weights = jnp.where(live, jnp.exp(scores - block_max[..., None]), 0.0)
        block_sum = lax.optimization_barrier(jnp.sum(weights, axis=-1))
        rounded = lax.optimization_barrier(weights.astype(jnp.bfloat16)).astype(jnp.float32)
        block_out = jnp.einsum('rcgek,rkgh->rcgeh', rounded, value_all)
        block_out = lax.optimization_barrier(block_out.astype(jnp.bfloat16)).astype(jnp.float32)
        return (block_max, block_sum, block_out)

    def advance(state_now, block_id):
        running_max, running_sum, summed = state_now
        block_max, block_sum, block_out = block_terms(block_id)
        new_max = jnp.maximum(running_max, block_max)
        old_factor = jnp.exp(running_max - new_max)
        new_factor = jnp.exp(block_max - new_max)
        return ((new_max, running_sum * old_factor + block_sum * new_factor, summed * old_factor[..., None] + block_out * new_factor[..., None]), None)
    start_state = (jnp.full((REQS, SPAN, KV_HEADS, group_size), MASKED, jnp.float32), jnp.zeros((REQS, SPAN, KV_HEADS, group_size), jnp.float32), jnp.zeros((REQS, SPAN, KV_HEADS, group_size, HEAD), jnp.float32))
    final_state, _ = lax.scan(advance, start_state, jnp.arange(N_SEQ, dtype=jnp.int32))
    running_max, running_sum, summed = final_state
    attended = (summed / running_sum[..., None]).reshape(REQS, SPAN, HEADS * HEAD).astype(jnp.bfloat16)
    return (attended, new_keys, new_values)
```

```python
import functools

import jax
import jax.numpy as jnp
import numpy as np
from jax import lax
from jax.experimental import pallas as pl
from jax.experimental.pallas import tpu as pltpu
from jax.sharding import PartitionSpec as P

HEADS = 4
KV_HEADS = 2
HEAD = 256


EPSILON = 1e-06
THETA = 1000042.0
MASKED = -1e30


def tables(positions, head_size):
    half_size = head_size // 2
    frequency = THETA ** (-(jnp.arange(half_size, dtype=jnp.float32) * 2.0 / head_size))
    angles = positions.astype(jnp.float32)[..., None] * frequency
    return (jnp.cos(angles)[..., None, :], jnp.sin(angles)[..., None, :])


def rotate(values, cosine, sine_part):
    half_size = values.shape[-1] // 2
    first_half = values[..., :half_size]
    second_half = values[..., half_size:]
    return jnp.concatenate(
        [
            first_half * cosine - second_half * sine_part,
            second_half * cosine + first_half * sine_part,
        ],
        axis=-1,
    )


def attend(query_rows, key_rows, value_rows, live):
    span_len = query_rows.shape[0]
    group_size = HEADS // KV_HEADS
    query_view = query_rows.reshape(span_len, KV_HEADS, group_size, HEAD)
    key_view = key_rows.reshape(key_rows.shape[0], KV_HEADS, HEAD)
    value_view = value_rows.reshape(value_rows.shape[0], KV_HEADS, HEAD)
    scores = jnp.einsum(
        "cgeh,kgh->cgek", query_view, key_view, preferred_element_type=jnp.float32
    ) * HEAD ** (-0.5)
    mask_view = live[:, None, None, :]
    scores = jnp.where(mask_view, scores, MASKED)
    block_max = jnp.max(scores, axis=-1)
    weights = jnp.where(mask_view, jnp.exp(scores - block_max[..., None]), 0.0)
    block_sum = jnp.sum(weights, axis=-1)
    block_out = jnp.einsum(
        "cgek,kgh->cgeh",
        weights.astype(jnp.bfloat16),
        value_view,
        preferred_element_type=jnp.float32,
    )
    return (
        block_max.reshape(span_len, HEADS),
        block_sum.reshape(span_len, HEADS),
        block_out.reshape(span_len, HEADS * HEAD).astype(jnp.bfloat16),
    )


def attend_rows(query_rows, key_rows, value_rows, live):
    total_rows = query_rows.shape[0]
    row_block = min(512, total_rows)
    pieces = []
    for begin in range(0, total_rows, row_block):
        pieces.append(
            attend(
                query_rows[begin : begin + row_block],
                key_rows,
                value_rows,
                live[begin : begin + row_block],
            )
        )
    return tuple((jnp.concatenate([piece[slot] for piece in pieces], axis=0) for slot in range(3)))


def body(hidden_in, norm_gain, w_query, w_key, w_value, cache_keys, cache_values, cache_lengths):
    seq_count = lax.axis_size("seq")
    seq_seat = lax.axis_index("seq")
    req_local, slice_len, model_width = hidden_in.shape
    cache_len_dev = cache_keys.shape[1]
    span_len = slice_len * seq_count
    inputs = hidden_in.astype(jnp.float32)
    normed = (
        inputs * lax.rsqrt(jnp.mean(inputs * inputs, axis=-1, keepdims=True) + EPSILON) * norm_gain
    ).astype(jnp.bfloat16)
    flat_rows = normed.reshape(req_local * slice_len, model_width)
    full_query, full_key, full_value = (
        lax.all_gather(w_query, ("req", "seq"), axis=0, tiled=True),
        lax.all_gather(w_key, ("req", "seq"), axis=0, tiled=True),
        lax.all_gather(w_value, ("req", "seq"), axis=0, tiled=True),
    )
    query_raw = jnp.dot(flat_rows, full_query, preferred_element_type=jnp.float32)
    key_raw = jnp.dot(flat_rows, full_key, preferred_element_type=jnp.float32)
    value_raw = jnp.dot(flat_rows, full_value, preferred_element_type=jnp.float32)
    local_index = jnp.arange(slice_len, dtype=jnp.int32)
    positions = cache_lengths[:, None] + seq_seat * slice_len + local_index[None, :]
    cosine, sine_part = tables(positions, HEAD)
    queries = (
        rotate(query_raw.reshape(req_local, slice_len, HEADS, HEAD), cosine, sine_part)
        .reshape(req_local, slice_len, HEADS * HEAD)
        .astype(jnp.bfloat16)
    )
    new_keys = (
        rotate(key_raw.reshape(req_local, slice_len, KV_HEADS, HEAD), cosine, sine_part)
        .reshape(req_local, slice_len, KV_HEADS * HEAD)
        .astype(jnp.bfloat16)
    )
    new_values = value_raw.reshape(req_local, slice_len, KV_HEADS * HEAD).astype(jnp.bfloat16)
    all_queries = lax.all_gather(queries, "seq", axis=1, tiled=True)
    key_block = jnp.concatenate([cache_keys, new_keys], axis=1)
    value_block = jnp.concatenate([cache_values, new_values], axis=1)
    span_index = jnp.arange(span_len, dtype=jnp.int32)
    cache_pos = seq_seat * cache_len_dev + jnp.arange(cache_len_dev, dtype=jnp.int32)
    new_pos = seq_seat * slice_len + local_index
    new_live = new_pos[None, :] <= span_index[:, None]
    max_list = []
    sum_list = []
    out_list = []
    for request in range(req_local):
        cache_live = cache_pos < cache_lengths[request]
        live_full = jnp.concatenate(
            [jnp.broadcast_to(cache_live[None, :], (span_len, cache_len_dev)), new_live], axis=1
        )
        query_rows = all_queries[request]
        terms = attend_rows(query_rows, key_block[request], value_block[request], live_full)
        max_list.append(terms[0])
        sum_list.append(terms[1])
        out_list.append(terms[2])
    max_all = jnp.stack(max_list)
    sum_all = jnp.stack(sum_list)
    out_all = jnp.stack(out_list)
    got_max, got_sum = (
        lax.all_to_all(max_all, "seq", split_axis=1, concat_axis=0, tiled=True),
        lax.all_to_all(sum_all, "seq", split_axis=1, concat_axis=0, tiled=True),
    )
    got_out = lax.all_to_all(out_all, "seq", split_axis=1, concat_axis=0, tiled=True)
    got_max = got_max.reshape(seq_count, req_local, slice_len, HEADS)
    got_sum = got_sum.reshape(seq_count, req_local, slice_len, HEADS)
    got_out = got_out.reshape(seq_count, req_local, slice_len, HEADS, HEAD)
    best_max = jnp.max(got_max, axis=0)
    factor = jnp.exp(got_max - best_max)
    total_sum = jnp.sum(got_sum * factor, axis=0)
    total_out = jnp.sum(got_out.astype(jnp.float32) * factor[..., None], axis=0)
    attended = (
        (total_out / total_sum[..., None])
        .reshape(req_local, slice_len, HEADS * HEAD)
        .astype(jnp.bfloat16)
    )
    return (attended, new_keys, new_values)

MESH_ID = pl.DeviceIdType.MESH


def fused_kernel(
    planes,
    x_hbm,
    gain_ref,
    freq_ref,
    wq,
    wk,
    wv,
    ck,
    cv,
    lens,
    att,
    nk,
    nv,
    xin,
    xbuf,
    wbuf,
    kvbuf,
    stage,
    nbuf,
    ostage,
    sbuf,
    cos_t,
    sin_t,
    xin_sem,
    w_send,
    w_recv,
    z_send,
    z_recv,
    x_send,
    x_recv,
    c_send,
    c_recv,
    f_send,
    f_recv,
    n_send,
    n_recv,
    o_send,
    o_recv,
    a_send,
    a_recv,
):
    me = lax.axis_index("seq")
    plane = lax.axis_index("req")
    chip, core = lax.div(me, 2), lax.rem(me, 2)
    group, lane = lax.div(chip, 2), lax.rem(chip, 2)
    sibling = chip * 2 + (1 - core)
    slice_len = xin.shape[1]
    span = slice_len * 8
    w_rows = wq.shape[0]
    block = ck.shape[1]
    depth = w_rows * 8

    def cols(index):
        return pl.ds(pl.multiple_of(index * HEAD, HEAD), HEAD)

    def remote(src, dst, ssem, rsem, peer):
        return pltpu.make_async_remote_copy(
            src_ref=src,
            dst_ref=dst,
            send_sem=ssem,
            recv_sem=rsem,
            device_id={"seq": peer},
            device_id_type=MESH_ID,
        )

    def push(src, dst, ssem, rsem, peer):
        @pl.when(peer != me)
        def _():
            remote(src, dst, ssem, rsem, peer).start()

        @pl.when(peer == me)
        def _():
            pltpu.make_async_copy(src, dst, rsem).start()

    def drain(src, dst, ssem, rsem, peer):
        @pl.when(peer != me)
        def _():
            remote(src, dst, ssem, rsem, peer).wait_send()

    def arrived(dst, rsem):
        pltpu.make_async_copy(dst, dst, rsem).wait()

    load_x = pltpu.make_async_copy(x_hbm, xin, xin_sem)
    load_x.start()
    barrier = pltpu.get_barrier_semaphore()
    for d in range(1, 8):
        pl.semaphore_signal(
            barrier, inc=1, device_id={"seq": lax.rem(me + d, 8)}, device_id_type=MESH_ID
        )
    for d in range(1, planes):
        pl.semaphore_signal(
            barrier, inc=1, device_id={"req": lax.rem(plane + d, planes)}, device_id_type=MESH_ID
        )
    load_x.wait()
    rows = xin[...].astype(jnp.float32)
    mean = jnp.mean(rows * rows, axis=-1, keepdims=True)
    normed = (rows * lax.rsqrt(mean + EPSILON) * gain_ref[...][None]).astype(jnp.bfloat16)
    xbuf[:, pl.ds(pl.multiple_of(me * slice_len, slice_len), slice_len), :] = normed
    pl.semaphore_wait(barrier, 7 + planes - 1)

    def w_slot(source):
        return wbuf.at[plane, pl.ds(pl.multiple_of(source * w_rows, w_rows), w_rows), :]

    for d in list(range(1, 8)) + [0]:
        peer = lax.rem(me + d, 8)
        p_chip, p_core = lax.div(peer, 2), lax.rem(peer, 2)
        p_group, p_lane = lax.div(p_chip, 2), lax.rem(p_chip, 2)

        @pl.when(p_core == 0)
        def _():
            push(wq.at[:, cols(p_chip)], w_slot(me), w_send.at[d], w_recv.at[me], peer)

        @pl.when(p_core == 1)
        def _():
            @pl.when(p_lane == 0)
            def _():
                push(wk.at[:, cols(p_group)], w_slot(me), w_send.at[d], w_recv.at[me], peer)

            @pl.when(p_lane == 1)
            def _():
                push(wv.at[:, cols(p_group)], w_slot(me), w_send.at[d], w_recv.at[me], peer)

    def x_slot(source):
        return xbuf.at[:, pl.ds(pl.multiple_of(source * slice_len, slice_len), slice_len), :]

    def x_copy(d):
        peer = lax.rem(chip + d, 4) * 2 + core if d else sibling
        return remote(x_slot(me), x_slot(me), x_send.at[d], x_recv.at[me], peer)

    def x_forward(d):
        source = lax.rem(chip + 4 - d, 4) * 2 + core
        return source, remote(
            x_slot(source), x_slot(source), x_send.at[3 + d], x_recv.at[source], sibling
        )

    for d in (1, 2, 3, 0):
        x_copy(d).start()

    def c_slot(which, source):
        return kvbuf.at[which, pl.ds(pl.multiple_of(source * block, block), block), :]

    for d in list(range(1, 8)) + [0]:
        peer = lax.rem(me + d, 8)
        p_chip, p_core = lax.div(peer, 2), lax.rem(peer, 2)
        p_group, p_lane = lax.div(p_chip, 2), lax.rem(p_chip, 2)

        @pl.when(p_core == 0)
        def _():
            push(ck.at[p_lane, :, cols(p_group)], c_slot(0, me), c_send.at[d], c_recv.at[me], peer)

        @pl.when(p_core == 1)
        def _():
            push(cv.at[p_lane, :, cols(p_group)], c_slot(1, me), c_send.at[d], c_recv.at[me], peer)

    for s in range(8):
        arrived(w_slot(s), w_recv.at[s])

    def z_copy(d):
        return pltpu.make_async_remote_copy(
            src_ref=wbuf.at[plane],
            dst_ref=wbuf.at[plane],
            send_sem=z_send.at[d],
            recv_sem=z_recv.at[plane],
            device_id={"req": lax.rem(plane + d, planes)},
            device_id_type=MESH_ID,
        )

    for d in range(1, planes):
        z_copy(d).start()

    is_value = core * lane
    turn = (1 - is_value).astype(jnp.float32)
    for r in range(2):
        position = lens[r] + lax.broadcasted_iota(jnp.int32, (span, HEAD // 2), 0)
        angle = position.astype(jnp.float32) * freq_ref[...] * turn
        cos_t[r] = jnp.cos(angle)
        sin_t[r] = jnp.sin(angle)

    for d in range(1, 4):
        source, forward = x_forward(d)
        arrived(x_slot(source), x_recv.at[source])
        forward.start()
    arrived(x_slot(sibling), x_recv.at[sibling])
    for d in range(1, 4):
        source = lax.rem(chip + 4 - d, 4) * 2 + (1 - core)
        arrived(x_slot(source), x_recv.at[source])

    def product(index):
        part = xbuf[:, :, pl.ds(pl.multiple_of(index * depth, depth), depth)]
        return jnp.dot(
            part.reshape(2 * span, depth), wbuf[index], preferred_element_type=jnp.float32
        )

    total = product(plane)

    def c_forward(d):
        source = lax.rem(me + 8 - d, 8)
        slot = c_slot(core, source)
        return source, slot, remote(slot, slot, f_send.at[d], f_recv.at[source], sibling)

    for d in [0] + list(range(1, 8)):
        source, slot, forward = c_forward(d)
        arrived(slot, c_recv.at[source])
        forward.start()

    for d in range(1, planes):
        source = lax.rem(plane + d, planes)
        arrived(wbuf.at[source], z_recv.at[source])
        total = total + product(source)

    half = HEAD // 2
    for r in range(2):
        first = total[r * span : (r + 1) * span, :half]
        second = total[r * span : (r + 1) * span, half:]
        cosine, sine = cos_t[r], sin_t[r]
        stage[r, :, :half] = (first * cosine - second * sine).astype(jnp.bfloat16)
        stage[r, :, half:] = (second * cosine + first * sine).astype(jnp.bfloat16)

    def exchange(act):
        @pl.when(core == 0)
        def _():
            for r in range(2):
                act(
                    stage.at[r],
                    nbuf.at[0],
                    n_send.at[r],
                    n_recv.at[0],
                    (2 * group + r) * 2 + lane,
                )

        @pl.when(core == 1)
        def _():
            for r in range(2):
                for k in range(2):
                    act(
                        stage.at[r],
                        nbuf.at[1 + lane],
                        n_send.at[2 * r + k],
                        n_recv.at[1 + lane],
                        (2 * group + r) * 2 + k,
                    )

    def new_rows(act):
        @pl.when(core == 1)
        def _():
            for which, out in ((0, nk), (1, nv)):

                @pl.when(lane == which)
                def _():
                    for d in range(8):
                        peer = lax.rem(me + d, 8)
                        begin = pl.multiple_of(peer * slice_len, slice_len)
                        act(
                            stage.at[:, pl.ds(begin, slice_len), :],
                            out.at[:, :, cols(group)],
                            o_send.at[d],
                            o_recv.at[2 * which + group],
                            peer,
                        )

    exchange(push)
    new_rows(push)

    length = lens[lane]
    arrived(nbuf.at[0], n_recv.at[0])
    queries = nbuf[0]
    contract = (((1,), (1,)), ((), ()))
    scale = HEAD ** (-0.5)
    for s in range(8):
        arrived(c_slot(1 - core, s), f_recv.at[s])
    top = jnp.full((span, 1), MASKED, jnp.float32)
    for s in range(8):
        scores = scale * lax.dot_general(
            queries,
            kvbuf[0, s * block : (s + 1) * block, :],
            contract,
            preferred_element_type=jnp.float32,
        )
        spot = s * block + lax.broadcasted_iota(jnp.int32, (span, block), 1)
        scores = jnp.where(spot < length, scores, MASKED)
        sbuf[s] = scores
        top = jnp.maximum(top, jnp.max(scores, axis=-1, keepdims=True))
    arrived(nbuf.at[1], n_recv.at[1])
    scores = scale * lax.dot_general(
        queries, nbuf[1], contract, preferred_element_type=jnp.float32
    )
    live = lax.broadcasted_iota(jnp.int32, (span, span), 1) <= lax.broadcasted_iota(
        jnp.int32, (span, span), 0
    )
    scores = jnp.where(live, scores, MASKED)
    top = jnp.maximum(top, jnp.max(scores, axis=-1, keepdims=True))
    weights = jnp.exp(scores - top)
    sums = jnp.sum(weights, axis=-1, keepdims=True)
    arrived(nbuf.at[2], n_recv.at[2])
    summed = jnp.dot(weights.astype(jnp.bfloat16), nbuf[2], preferred_element_type=jnp.float32)
    for s in range(8):
        weights = jnp.exp(sbuf[s] - top)
        sums = sums + jnp.sum(weights, axis=-1, keepdims=True)
        summed = summed + jnp.dot(
            weights.astype(jnp.bfloat16),
            kvbuf[1, s * block : (s + 1) * block, :],
            preferred_element_type=jnp.float32,
        )
    ostage[...] = (summed / sums).astype(jnp.bfloat16)

    def attended(act):
        for d in list(range(1, 8)) + [0]:
            peer = lax.rem(me + d, 8)
            begin = pl.multiple_of(peer * slice_len, slice_len)
            act(
                ostage.at[pl.ds(begin, slice_len), :],
                att.at[lane, :, cols(2 * group + core)],
                a_send.at[d],
                a_recv.at[me],
                peer,
            )

    attended(push)

    for d in range(1, 8):
        peer = lax.rem(me + d, 8)
        drain(w_slot(me), w_slot(me), w_send.at[d], w_recv.at[me], peer)
        drain(c_slot(0, me), c_slot(0, me), c_send.at[d], c_recv.at[me], peer)
    for d in range(1, planes):
        z_copy(d).wait_send()
    for d in range(4):
        x_copy(d).wait_send()
    for d in range(1, 4):
        x_forward(d)[1].wait_send()
    for d in range(8):
        c_forward(d)[2].wait_send()
    exchange(drain)
    new_rows(drain)
    attended(drain)
    for which, out in ((0, nk), (1, nv)):
        for g in range(2):
            arrived(out.at[:, :, g * HEAD : (g + 1) * HEAD], o_recv.at[2 * which + g])
    for s in range(8):
        s_chip = s // 2
        head = s_chip // 2 * 2 + s % 2
        arrived(att.at[s_chip % 2, :, head * HEAD : (head + 1) * HEAD], a_recv.at[s])


def fused_body(
    planes, hidden_in, norm_gain, w_query, w_key, w_value, cache_keys, cache_values, cache_lengths
):
    requests, slice_len, width = hidden_in.shape
    block = cache_keys.shape[1]
    span = slice_len * 8
    w_rows = w_query.shape[0]
    frequency = (THETA ** (-(np.arange(HEAD // 2) * 2.0 / HEAD))).astype(np.float32)[None]
    vmem = pl.BlockSpec(memory_space=pltpu.VMEM)
    hbm = pl.BlockSpec(memory_space=pl.ANY)
    smem = pl.BlockSpec(memory_space=pltpu.SMEM)
    dma = pltpu.SemaphoreType.DMA
    half = jnp.bfloat16
    return tuple(
        pl.pallas_call(
            functools.partial(fused_kernel, planes),
            out_shape=(
                jax.ShapeDtypeStruct((requests, slice_len, HEADS * HEAD), half),
                jax.ShapeDtypeStruct((requests, slice_len, KV_HEADS * HEAD), half),
                jax.ShapeDtypeStruct((requests, slice_len, KV_HEADS * HEAD), half),
            ),
            in_specs=[hbm, vmem, vmem, hbm, hbm, hbm, hbm, hbm, smem],
            out_specs=(hbm, hbm, hbm),
            scratch_shapes=[
                pltpu.VMEM((requests, slice_len, width), half),
                pltpu.VMEM((requests, span, width), half),
                pltpu.VMEM((planes, 8 * w_rows, HEAD), half),
                pltpu.VMEM((2, 8 * block, HEAD), half),
                pltpu.VMEM((requests, span, HEAD), half),
                pltpu.VMEM((3, span, HEAD), half),
                pltpu.VMEM((span, HEAD), half),
                pltpu.VMEM((8, span, block), jnp.float32),
                pltpu.VMEM((requests, span, HEAD // 2), jnp.float32),
                pltpu.VMEM((requests, span, HEAD // 2), jnp.float32),
                dma,
                dma((8,)),
                dma((8,)),
                dma((planes,)),
                dma((planes,)),
                dma((7,)),
                dma((8,)),
                dma((8,)),
                dma((8,)),
                dma((8,)),
                dma((8,)),
                dma((4,)),
                dma((3,)),
                dma((8,)),
                dma((4,)),
                dma((8,)),
                dma((8,)),
            ],
            compiler_params=pltpu.CompilerParams(
                collective_id=0, has_side_effects=True, vmem_limit_bytes=40 * 1024 * 1024
            ),
        )(
            hidden_in,
            norm_gain[None],
            jnp.asarray(frequency),
            w_query,
            w_key,
            w_value,
            cache_keys,
            cache_values,
            cache_lengths,
        )
    )


def solution(mesh):
    in_specs = (
        P("req", "seq", None),
        P(),
        P(("req", "seq"), None),
        P(("req", "seq"), None),
        P(("req", "seq"), None),
        P("req", "seq", None),
        P("req", "seq", None),
        P("req"),
    )
    out_specs = (P("req", "seq", None), P("req", "seq", None), P("req", "seq", None))
    program = body
    if mesh.shape["seq"] == HEADS + 2 * KV_HEADS:
        program = functools.partial(fused_body, mesh.shape["req"])
    return jax.shard_map(program, mesh=mesh, in_specs=in_specs, out_specs=out_specs, check_vma=False)
```

```python
import functools

import jax
import jax.numpy as jnp
import numpy as np
from jax import lax
from jax.experimental import pallas as pl
from jax.experimental.pallas import tpu as pltpu
from jax.sharding import PartitionSpec as P

HEADS = 4
KV_HEADS = 2
HEAD = 256


EPSILON = 1e-06
THETA = 1000042.0
MASKED = -1e30


def tables(positions, head_size):
    half_size = head_size // 2
    frequency = THETA ** (-(jnp.arange(half_size, dtype=jnp.float32) * 2.0 / head_size))
    angles = positions.astype(jnp.float32)[..., None] * frequency
    return (jnp.cos(angles)[..., None, :], jnp.sin(angles)[..., None, :])


def rotate(values, cosine, sine_part):
    half_size = values.shape[-1] // 2
    first_half = values[..., :half_size]
    second_half = values[..., half_size:]
    return jnp.concatenate(
        [
            first_half * cosine - second_half * sine_part,
            second_half * cosine + first_half * sine_part,
        ],
        axis=-1,
    )


def attend(query_rows, key_rows, value_rows, live):
    span_len = query_rows.shape[0]
    group_size = HEADS // KV_HEADS
    query_view = query_rows.reshape(span_len, KV_HEADS, group_size, HEAD)
    key_view = key_rows.reshape(key_rows.shape[0], KV_HEADS, HEAD)
    value_view = value_rows.reshape(value_rows.shape[0], KV_HEADS, HEAD)
    scores = jnp.einsum(
        "cgeh,kgh->cgek", query_view, key_view, preferred_element_type=jnp.float32
    ) * HEAD ** (-0.5)
    mask_view = live[:, None, None, :]
    scores = jnp.where(mask_view, scores, MASKED)
    block_max = jnp.max(scores, axis=-1)
    weights = jnp.where(mask_view, jnp.exp(scores - block_max[..., None]), 0.0)
    block_sum = jnp.sum(weights, axis=-1)
    block_out = jnp.einsum(
        "cgek,kgh->cgeh",
        weights.astype(jnp.bfloat16),
        value_view,
        preferred_element_type=jnp.float32,
    )
    return (
        block_max.reshape(span_len, HEADS),
        block_sum.reshape(span_len, HEADS),
        block_out.reshape(span_len, HEADS * HEAD).astype(jnp.bfloat16),
    )


def attend_rows(query_rows, key_rows, value_rows, live):
    total_rows = query_rows.shape[0]
    row_block = min(512, total_rows)
    pieces = []
    for begin in range(0, total_rows, row_block):
        pieces.append(
            attend(
                query_rows[begin : begin + row_block],
                key_rows,
                value_rows,
                live[begin : begin + row_block],
            )
        )
    return tuple((jnp.concatenate([piece[slot] for piece in pieces], axis=0) for slot in range(3)))


def body(hidden_in, norm_gain, w_query, w_key, w_value, cache_keys, cache_values, cache_lengths):
    seq_count = lax.axis_size("seq")
    seq_seat = lax.axis_index("seq")
    req_local, slice_len, model_width = hidden_in.shape
    cache_len_dev = cache_keys.shape[1]
    span_len = slice_len * seq_count
    inputs = hidden_in.astype(jnp.float32)
    normed = (
        inputs * lax.rsqrt(jnp.mean(inputs * inputs, axis=-1, keepdims=True) + EPSILON) * norm_gain
    ).astype(jnp.bfloat16)
    flat_rows = normed.reshape(req_local * slice_len, model_width)
    full_query, full_key, full_value = (
        lax.all_gather(w_query, ("req", "seq"), axis=0, tiled=True),
        lax.all_gather(w_key, ("req", "seq"), axis=0, tiled=True),
        lax.all_gather(w_value, ("req", "seq"), axis=0, tiled=True),
    )
    query_raw = jnp.dot(flat_rows, full_query, preferred_element_type=jnp.float32)
    key_raw = jnp.dot(flat_rows, full_key, preferred_element_type=jnp.float32)
    value_raw = jnp.dot(flat_rows, full_value, preferred_element_type=jnp.float32)
    local_index = jnp.arange(slice_len, dtype=jnp.int32)
    positions = cache_lengths[:, None] + seq_seat * slice_len + local_index[None, :]
    cosine, sine_part = tables(positions, HEAD)
    queries = (
        rotate(query_raw.reshape(req_local, slice_len, HEADS, HEAD), cosine, sine_part)
        .reshape(req_local, slice_len, HEADS * HEAD)
        .astype(jnp.bfloat16)
    )
    new_keys = (
        rotate(key_raw.reshape(req_local, slice_len, KV_HEADS, HEAD), cosine, sine_part)
        .reshape(req_local, slice_len, KV_HEADS * HEAD)
        .astype(jnp.bfloat16)
    )
    new_values = value_raw.reshape(req_local, slice_len, KV_HEADS * HEAD).astype(jnp.bfloat16)
    all_queries = lax.all_gather(queries, "seq", axis=1, tiled=True)
    key_block = jnp.concatenate([cache_keys, new_keys], axis=1)
    value_block = jnp.concatenate([cache_values, new_values], axis=1)
    span_index = jnp.arange(span_len, dtype=jnp.int32)
    cache_pos = seq_seat * cache_len_dev + jnp.arange(cache_len_dev, dtype=jnp.int32)
    new_pos = seq_seat * slice_len + local_index
    new_live = new_pos[None, :] <= span_index[:, None]
    max_list = []
    sum_list = []
    out_list = []
    for request in range(req_local):
        cache_live = cache_pos < cache_lengths[request]
        live_full = jnp.concatenate(
            [jnp.broadcast_to(cache_live[None, :], (span_len, cache_len_dev)), new_live], axis=1
        )
        query_rows = all_queries[request]
        terms = attend_rows(query_rows, key_block[request], value_block[request], live_full)
        max_list.append(terms[0])
        sum_list.append(terms[1])
        out_list.append(terms[2])
    max_all = jnp.stack(max_list)
    sum_all = jnp.stack(sum_list)
    out_all = jnp.stack(out_list)
    got_max, got_sum = (
        lax.all_to_all(max_all, "seq", split_axis=1, concat_axis=0, tiled=True),
        lax.all_to_all(sum_all, "seq", split_axis=1, concat_axis=0, tiled=True),
    )
    got_out = lax.all_to_all(out_all, "seq", split_axis=1, concat_axis=0, tiled=True)
    got_max = got_max.reshape(seq_count, req_local, slice_len, HEADS)
    got_sum = got_sum.reshape(seq_count, req_local, slice_len, HEADS)
    got_out = got_out.reshape(seq_count, req_local, slice_len, HEADS, HEAD)
    best_max = jnp.max(got_max, axis=0)
    factor = jnp.exp(got_max - best_max)
    total_sum = jnp.sum(got_sum * factor, axis=0)
    total_out = jnp.sum(got_out.astype(jnp.float32) * factor[..., None], axis=0)
    attended = (
        (total_out / total_sum[..., None])
        .reshape(req_local, slice_len, HEADS * HEAD)
        .astype(jnp.bfloat16)
    )
    return (attended, new_keys, new_values)

MESH_ID = pl.DeviceIdType.MESH


def fused_kernel(
    planes,
    x_hbm,
    gain_hbm,
    freq_hbm,
    wq,
    wk,
    wv,
    ck,
    cv,
    lens,
    att,
    nk,
    nv,
    gain_ref,
    freq_ref,
    xin,
    xbuf,
    wbuf,
    kvbuf,
    stage,
    nbuf,
    ostage,
    sbuf,
    cos_t,
    sin_t,
    xin_sem,
    w_send,
    w_recv,
    z_send,
    z_recv,
    x_send,
    x_recv,
    c_send,
    c_recv,
    f_send,
    f_recv,
    n_send,
    n_recv,
    o_send,
    o_recv,
    a_send,
    a_recv,
):
    me = lax.axis_index("seq")
    plane = lax.axis_index("req")
    chip, core = lax.div(me, 2), lax.rem(me, 2)
    group, lane = lax.div(chip, 2), lax.rem(chip, 2)
    sibling = chip * 2 + (1 - core)
    slice_len = xin.shape[1]
    span = slice_len * 8
    w_rows = wq.shape[0]
    block = ck.shape[1]
    depth = w_rows * 8

    def cols(index):
        return pl.ds(pl.multiple_of(index * HEAD, HEAD), HEAD)

    def remote(src, dst, ssem, rsem, peer):
        return pltpu.make_async_remote_copy(
            src_ref=src,
            dst_ref=dst,
            send_sem=ssem,
            recv_sem=rsem,
            device_id={"seq": peer},
            device_id_type=MESH_ID,
        )

    def push(src, dst, ssem, rsem, peer):
        @pl.when(peer != me)
        def _():
            remote(src, dst, ssem, rsem, peer).start()

        @pl.when(peer == me)
        def _():
            pltpu.make_async_copy(src, dst, rsem).start()

    def drain(src, dst, ssem, rsem, peer):
        @pl.when(peer != me)
        def _():
            remote(src, dst, ssem, rsem, peer).wait_send()

    def arrived(dst, rsem):
        pltpu.make_async_copy(dst, dst, rsem).wait()

    loads = [
        pltpu.make_async_copy(source, target, xin_sem.at[index])
        for index, (source, target) in enumerate(
            ((x_hbm, xin), (gain_hbm, gain_ref), (freq_hbm, freq_ref))
        )
    ]
    for load in loads:
        load.start()
    barrier = pltpu.get_barrier_semaphore()
    for d in range(1, 8):
        pl.semaphore_signal(
            barrier, inc=1, device_id={"seq": lax.rem(me + d, 8)}, device_id_type=MESH_ID
        )
    for d in range(1, planes):
        pl.semaphore_signal(
            barrier, inc=1, device_id={"req": lax.rem(plane + d, planes)}, device_id_type=MESH_ID
        )
    for load in loads:
        load.wait()
    rows = xin[...].astype(jnp.float32)
    mean = jnp.mean(rows * rows, axis=-1, keepdims=True)
    normed = (rows * lax.rsqrt(mean + EPSILON) * gain_ref[...][None]).astype(jnp.bfloat16)
    xbuf[:, pl.ds(pl.multiple_of(me * slice_len, slice_len), slice_len), :] = normed
    pl.semaphore_wait(barrier, 7 + planes - 1)

    def w_slot(source):
        return wbuf.at[plane, pl.ds(pl.multiple_of(source * w_rows, w_rows), w_rows), :]

    for d in list(range(1, 8)) + [0]:
        peer = lax.rem(me + d, 8)
        p_chip, p_core = lax.div(peer, 2), lax.rem(peer, 2)
        p_group, p_lane = lax.div(p_chip, 2), lax.rem(p_chip, 2)

        @pl.when(p_core == 0)
        def _():
            push(wq.at[:, cols(p_chip)], w_slot(me), w_send.at[d], w_recv.at[me], peer)

        @pl.when(p_core == 1)
        def _():
            @pl.when(p_lane == 0)
            def _():
                push(wk.at[:, cols(p_group)], w_slot(me), w_send.at[d], w_recv.at[me], peer)

            @pl.when(p_lane == 1)
            def _():
                push(wv.at[:, cols(p_group)], w_slot(me), w_send.at[d], w_recv.at[me], peer)

    def x_slot(source):
        return xbuf.at[:, pl.ds(pl.multiple_of(source * slice_len, slice_len), slice_len), :]

    beside, across, far = chip + 1 - 2 * lane, lax.rem(chip + 2, 4), 3 - chip

    def x_copy(d):
        peer = (sibling, beside * 2 + core, across * 2 + core)[d]
        return remote(x_slot(me), x_slot(me), x_send.at[d], x_recv.at[me], peer)

    def x_half(source, part):
        return xbuf.at[
            part, pl.ds(pl.multiple_of(source * slice_len, slice_len), slice_len), :
        ]

    def x_relay(d):
        source = (beside if d == 0 else across) * 2 + core
        peer = (across if d == 0 else beside) * 2 + core
        slot = x_half(source, d)
        return remote(slot, slot, x_send.at[3 + d], (x_recv.at[source], x_recv.at[8])[d], peer)

    def x_forward(d):
        source = (far, beside, across)[d] * 2 + core
        return source, remote(
            x_slot(source), x_slot(source), x_send.at[5 + d], x_recv.at[source], sibling
        )

    for d in (1, 2, 0):
        x_copy(d).start()

    def c_slot(which, source):
        return kvbuf.at[which, pl.ds(pl.multiple_of(source * block, block), block), :]

    for d in list(range(1, 8)) + [0]:
        peer = lax.rem(me + d, 8)
        p_chip, p_core = lax.div(peer, 2), lax.rem(peer, 2)
        p_group, p_lane = lax.div(p_chip, 2), lax.rem(p_chip, 2)

        @pl.when(p_core == 0)
        def _():
            push(ck.at[p_lane, :, cols(p_group)], c_slot(0, me), c_send.at[d], c_recv.at[me], peer)

        @pl.when(p_core == 1)
        def _():
            push(cv.at[p_lane, :, cols(p_group)], c_slot(1, me), c_send.at[d], c_recv.at[me], peer)

    for s in range(8):
        arrived(w_slot(s), w_recv.at[s])

    def z_copy(d):
        return pltpu.make_async_remote_copy(
            src_ref=wbuf.at[plane],
            dst_ref=wbuf.at[plane],
            send_sem=z_send.at[d],
            recv_sem=z_recv.at[plane],
            device_id={"req": lax.rem(plane + d, planes)},
            device_id_type=MESH_ID,
        )

    relayed = 3 * (2 - plane) if planes == 4 else planes

    def z_direct(act):
        for d in (2, 1, 3) if planes == 4 else range(1, planes):
            if planes == 4 and d != 2:

                @pl.when(lax.abs(lax.rem(plane + d, planes) - plane) != 3)
                def _():
                    act(z_copy(d))

            else:
                act(z_copy(d))

    def z_relay(act):
        if planes == 4:

            @pl.when((plane == 1) | (plane == 2))
            def _():
                act(
                    pltpu.make_async_remote_copy(
                        src_ref=wbuf.at[relayed],
                        dst_ref=wbuf.at[relayed],
                        send_sem=z_send.at[0],
                        recv_sem=z_recv.at[relayed],
                        device_id={"req": 3 - relayed},
                        device_id_type=MESH_ID,
                    )
                )

    def z_pass(copy):
        arrived(wbuf.at[relayed], z_recv.at[relayed])
        copy.start()

    z_direct(lambda copy: copy.start())

    is_value = core * lane
    turn = (1 - is_value).astype(jnp.float32)
    for r in range(2):
        position = lens[r] + lax.broadcasted_iota(jnp.int32, (span, HEAD // 2), 0)
        angle = position.astype(jnp.float32) * freq_ref[...] * turn
        cos_t[r] = jnp.cos(angle)
        sin_t[r] = jnp.sin(angle)

    for d in (1, 2):
        source, forward = x_forward(d)
        arrived(x_slot(source), x_recv.at[source])
        x_relay(d - 1).start()
        forward.start()
    z_relay(z_pass)
    source, forward = x_forward(0)
    arrived(x_half(source, 0), x_recv.at[source])
    arrived(x_half(source, 1), x_recv.at[8])
    forward.start()
    arrived(x_slot(sibling), x_recv.at[sibling])
    for d in range(1, 4):
        source = lax.rem(chip + 4 - d, 4) * 2 + (1 - core)
        arrived(x_slot(source), x_recv.at[source])

    def product(index):
        part = xbuf[:, :, pl.ds(pl.multiple_of(index * depth, depth), depth)]
        return jnp.dot(
            part.reshape(2 * span, depth), wbuf[index], preferred_element_type=jnp.float32
        )

    total = product(plane)

    def c_forward(d):
        source = lax.rem(me + 8 - d, 8)
        slot = c_slot(core, source)
        return source, slot, remote(slot, slot, f_send.at[d], f_recv.at[source], sibling)

    for d in [0] + list(range(1, 8)):
        source, slot, forward = c_forward(d)
        arrived(slot, c_recv.at[source])
        forward.start()

    for d in range(1, planes):
        source = lax.rem(plane + d, planes)

        @pl.when(source != relayed)
        def _():
            arrived(wbuf.at[source], z_recv.at[source])

        total = total + product(source)

    half = HEAD // 2
    for r in range(2):
        first = total[r * span : (r + 1) * span, :half]
        second = total[r * span : (r + 1) * span, half:]
        cosine, sine = cos_t[r], sin_t[r]
        stage[r, :, :half] = (first * cosine - second * sine).astype(jnp.bfloat16)
        stage[r, :, half:] = (second * cosine + first * sine).astype(jnp.bfloat16)

    def exchange(act):
        @pl.when(core == 0)
        def _():
            for r in range(2):
                act(
                    stage.at[r],
                    nbuf.at[0],
                    n_send.at[r],
                    n_recv.at[0],
                    (2 * group + r) * 2 + lane,
                )

        @pl.when(core == 1)
        def _():
            for r in range(2):
                for k in range(2):
                    act(
                        stage.at[r],
                        nbuf.at[1 + lane],
                        n_send.at[2 * r + k],
                        n_recv.at[1 + lane],
                        (2 * group + r) * 2 + k,
                    )

    def new_rows(act):
        @pl.when(core == 1)
        def _():
            for which, out in ((0, nk), (1, nv)):

                @pl.when(lane == which)
                def _():
                    for d in range(8):
                        peer = lax.rem(me + d, 8)
                        begin = pl.multiple_of(peer * slice_len, slice_len)
                        act(
                            stage.at[:, pl.ds(begin, slice_len), :],
                            out.at[:, :, cols(group)],
                            o_send.at[d],
                            o_recv.at[2 * which + group],
                            peer,
                        )

    exchange(push)

    length = lens[lane]
    arrived(nbuf.at[0], n_recv.at[0])
    queries = nbuf[0]
    contract = (((1,), (1,)), ((), ()))
    scale = HEAD ** (-0.5)
    for s in range(8):
        arrived(c_slot(1 - core, s), f_recv.at[s])
    top = jnp.full((span, 1), MASKED, jnp.float32)
    for s in range(8):
        scores = scale * lax.dot_general(
            queries,
            kvbuf[0, s * block : (s + 1) * block, :],
            contract,
            preferred_element_type=jnp.float32,
        )
        spot = s * block + lax.broadcasted_iota(jnp.int32, (span, block), 1)
        scores = jnp.where(spot < length, scores, MASKED)
        sbuf[s] = scores
        top = jnp.maximum(top, jnp.max(scores, axis=-1, keepdims=True))
    arrived(nbuf.at[1], n_recv.at[1])
    scores = scale * lax.dot_general(
        queries, nbuf[1], contract, preferred_element_type=jnp.float32
    )
    live = lax.broadcasted_iota(jnp.int32, (span, span), 1) <= lax.broadcasted_iota(
        jnp.int32, (span, span), 0
    )
    scores = jnp.where(live, scores, MASKED)
    top = jnp.maximum(top, jnp.max(scores, axis=-1, keepdims=True))
    weights = jnp.exp(scores - top)
    sums = jnp.sum(weights, axis=-1, keepdims=True)
    arrived(nbuf.at[2], n_recv.at[2])
    summed = jnp.dot(weights.astype(jnp.bfloat16), nbuf[2], preferred_element_type=jnp.float32)
    for s in range(8):
        weights = jnp.exp(sbuf[s] - top)
        sums = sums + jnp.sum(weights, axis=-1, keepdims=True)
        summed = summed + jnp.dot(
            weights.astype(jnp.bfloat16),
            kvbuf[1, s * block : (s + 1) * block, :],
            preferred_element_type=jnp.float32,
        )
    ostage[...] = (summed / sums).astype(jnp.bfloat16)

    def attended(act):
        for d in list(range(1, 8)) + [0]:
            peer = lax.rem(me + d, 8)
            begin = pl.multiple_of(peer * slice_len, slice_len)
            act(
                ostage.at[pl.ds(begin, slice_len), :],
                att.at[lane, :, cols(2 * group + core)],
                a_send.at[d],
                a_recv.at[me],
                peer,
            )

    attended(push)
    new_rows(push)

    for d in range(1, 8):
        peer = lax.rem(me + d, 8)
        drain(w_slot(me), w_slot(me), w_send.at[d], w_recv.at[me], peer)
        drain(c_slot(0, me), c_slot(0, me), c_send.at[d], c_recv.at[me], peer)
    z_direct(lambda copy: copy.wait_send())
    z_relay(lambda copy: copy.wait_send())
    for d in range(3):
        x_copy(d).wait_send()
        x_forward(d)[1].wait_send()
    for d in range(2):
        x_relay(d).wait_send()
    for d in range(8):
        c_forward(d)[2].wait_send()
    exchange(drain)
    new_rows(drain)
    attended(drain)
    for which, out in ((0, nk), (1, nv)):
        for g in range(2):
            arrived(out.at[:, :, g * HEAD : (g + 1) * HEAD], o_recv.at[2 * which + g])
    for s in range(8):
        s_chip = s // 2
        head = s_chip // 2 * 2 + s % 2
        arrived(att.at[s_chip % 2, :, head * HEAD : (head + 1) * HEAD], a_recv.at[s])


def fused_body(
    planes, hidden_in, norm_gain, w_query, w_key, w_value, cache_keys, cache_values, cache_lengths
):
    requests, slice_len, width = hidden_in.shape
    block = cache_keys.shape[1]
    span = slice_len * 8
    w_rows = w_query.shape[0]
    frequency = (THETA ** (-(np.arange(HEAD // 2) * 2.0 / HEAD))).astype(np.float32)[None]
    hbm = pl.BlockSpec(memory_space=pltpu.HBM)
    anywhere = pl.BlockSpec(memory_space=pl.ANY)
    smem = pl.BlockSpec(memory_space=pltpu.SMEM)
    dma = pltpu.SemaphoreType.DMA
    half = jnp.bfloat16
    return tuple(
        pl.pallas_call(
            functools.partial(fused_kernel, planes),
            out_shape=(
                jax.ShapeDtypeStruct((requests, slice_len, HEADS * HEAD), half),
                jax.ShapeDtypeStruct((requests, slice_len, KV_HEADS * HEAD), half),
                jax.ShapeDtypeStruct((requests, slice_len, KV_HEADS * HEAD), half),
            ),
            in_specs=[hbm, hbm, hbm, hbm, hbm, hbm, hbm, hbm, smem],
            out_specs=(anywhere, anywhere, anywhere),
            scratch_shapes=[
                pltpu.VMEM((1, width), jnp.float32),
                pltpu.VMEM((1, HEAD // 2), jnp.float32),
                pltpu.VMEM((requests, slice_len, width), half),
                pltpu.VMEM((requests, span, width), half),
                pltpu.VMEM((planes, 8 * w_rows, HEAD), half),
                pltpu.VMEM((2, 8 * block, HEAD), half),
                pltpu.VMEM((requests, span, HEAD), half),
                pltpu.VMEM((3, span, HEAD), half),
                pltpu.VMEM((span, HEAD), half),
                pltpu.VMEM((8, span, block), jnp.float32),
                pltpu.VMEM((requests, span, HEAD // 2), jnp.float32),
                pltpu.VMEM((requests, span, HEAD // 2), jnp.float32),
                dma((3,)),
                dma((8,)),
                dma((8,)),
                dma((planes,)),
                dma((planes,)),
                dma((8,)),
                dma((9,)),
                dma((8,)),
                dma((8,)),
                dma((8,)),
                dma((8,)),
                dma((4,)),
                dma((3,)),
                dma((8,)),
                dma((4,)),
                dma((8,)),
                dma((8,)),
            ],
            compiler_params=pltpu.CompilerParams(
                collective_id=0, has_side_effects=True, vmem_limit_bytes=64 * 1024 * 1024
            ),
        )(
            hidden_in,
            norm_gain[None],
            jnp.asarray(frequency),
            w_query,
            w_key,
            w_value,
            cache_keys,
            cache_values,
            cache_lengths,
        )
    )


def solution(mesh):
    in_specs = (
        P("req", "seq", None),
        P(),
        P(("req", "seq"), None),
        P(("req", "seq"), None),
        P(("req", "seq"), None),
        P("req", "seq", None),
        P("req", "seq", None),
        P("req"),
    )
    out_specs = (P("req", "seq", None), P("req", "seq", None), P("req", "seq", None))
    program = body
    if mesh.shape["seq"] == HEADS + 2 * KV_HEADS:
        program = functools.partial(fused_body, mesh.shape["req"])
    return jax.shard_map(program, mesh=mesh, in_specs=in_specs, out_specs=out_specs, check_vma=False)
```
